32 devices in a mesh: orient: 8 (over y, x, core), slab: 4 (over z).
Axes of the slice: x: 2, y: 2, z: 4, core: 2. Of those that a mesh axis runs over, the one named last changes fastest.
Arguments:
- images: bfloat16 [12288, 8192], P(('orient', 'slab')), may hold values from -20 to 20
- bucket: int32 [12288, 1], P(('orient', 'slab')), may hold values from 0 to 7; in each aligned block of 384 rows (0 to 383, 384 to 767, ...) at most 96 rows name the same one
- panels: bfloat16 [8, 512, 8192], P('orient'), may hold values from -6 to 6
- tile_slab: int32 [8, 64], replicated, may hold values from 0 to 3, as said below
- tile_row: int32 [8, 64], replicated, may hold values from 0 to 248
Outputs:
- volume: float32 [1024, 8192], P('slab', 'orient')
- loglik: float32 [12288], P(('orient', 'slab'))
The draws below stay inside these ranges and needn't reach their ends.
Inputs may be any that keep to these rules, and one draw needn't show every extreme that they name: Among the rows of one device, at most 96 particles name one bucket, a bound that some block reaches. `tile_slab`: for every bucket, at most 24 of its tiles name one slab, and some slab is named by exactly 24 of them.
All inputs are finite; a program needn't handle non-finite values.
Results may differ from the reference program's by a relative error of at most 0.0038.
Values may be sent and summed in bfloat16 or wider, within the bound.
No kernel may reach another device: no remote copies, remote signals or barrier semaphores. Data moves between devices by JAX's collectives and lax.ppermute only.
A program may use at most 128 MiB of HBM per device.

```python
import math
import jax
import jax.numpy as jnp
import numpy as np
from jax import lax

W = 8192
ORI = 512
G = 8
P_DEV = 384
SLAB_ROWS = 256
PARTS_SIZE = 12288
CAP = 96
TILES = 64
TCAP = 24
VROWS = 1024
N_ORIENT = 8
N_SLAB = 4


def draw_images(key, part):
    key = jax.random.fold_in(key, 11)
    first_key, second_key = jax.random.split(key)
    scales = jnp.exp(jax.random.uniform(first_key, (PARTS_SIZE, 1), minval=math.log(0.5), maxval=math.log(4.0)))
    values = scales * jnp.clip(jax.random.normal(second_key, (PARTS_SIZE, W)), -5.0, 5.0)
    return values.astype(jnp.bfloat16)


def draw_panels(key, part):
    key = jax.random.fold_in(key, 12)
    entries = jnp.clip(jax.random.normal(key, (N_ORIENT, ORI, W)), -5.0, 5.0)
    return entries.astype(jnp.bfloat16)


def draw_tile_slab(key, part):
    key = jax.random.fold_in(key, 13)

    def one_bucket(bucket_key):
        first_key, second_key, third_key = jax.random.split(bucket_key, 3)
        slot_total = N_SLAB * TCAP
        full_slab = jax.random.randint(first_key, (), 0, N_SLAB)
        shuffled = jax.random.permutation(second_key, slot_total)
        ranking = jnp.where(shuffled // TCAP == full_slab, 0, 1) * slot_total + jnp.arange(slot_total)
        leading = jnp.argsort(ranking)
        chosen = shuffled[leading][:TILES]
        slab_of = chosen // TCAP
        return jax.random.permutation(third_key, slab_of)
    return jax.vmap(one_bucket)(jax.random.split(key, N_ORIENT)).astype(jnp.int32)


def with_ends(drawn, own_key, least, high):
    shape = drawn.shape
    place = [jax.random.randint(jax.random.fold_in(own_key, axis), (), 0, shape[axis]) for axis in range(len(shape))]
    drawn = drawn.at[tuple(place)].set(least)
    longest = shape.index(max(shape))
    place[longest] = (place[longest] + 1) % shape[longest]
    return drawn.at[tuple(place)].set(high)


def assign_block(rng, own, number, rows, number_of, top, bound, lean):
    order = jax.random.permutation(rng, number_of)
    crowded, common = shares(number_of, rows * top, bound, lean, True), shares(number_of, rows * top, bound, lean, False)
    places = jnp.arange(number_of)

    def named(sizes, rotation):
        used = int((sizes > 0).sum())
        fixed = max(1, used // 4)
        shifted = fixed + (places - fixed + rotation * (used - fixed)) % max(1, number_of - fixed)
        return jnp.zeros((number_of,), jnp.int32).at[order[jnp.where(places < fixed, places, shifted)]].set(jnp.asarray(sizes, jnp.int32))

    sizes = jnp.where(number % 4 == 0, named(crowded, number // 4), named(common, number - number // 4 - 1))
    mixed = jax.random.permutation(jax.random.fold_in(own, 3), number_of)
    donor, sink = mixed[0:number_of // 2 * 2:2], mixed[1:number_of // 2 * 2:2]
    margin = jnp.minimum(sizes[donor] - 1, bound - sizes[sink]) // 2
    margin = jnp.where((donor == order[0]) | (sink == order[0]) | (sizes[sink] == 0), 0, jnp.maximum(margin, 0))
    shifted = jax.random.randint(jax.random.fold_in(own, 4), (number_of // 2,), 0, 1 << 20) % (margin + 1)
    sizes = sizes.at[donor].add(-shifted).at[sink].add(shifted)
    items = jnp.searchsorted(jnp.cumsum(sizes), jnp.arange(rows * top), side="right").astype(jnp.int32)
    listing = items.reshape(top, rows).T
    listing = listing[jax.random.permutation(jax.random.fold_in(own, 1), rows)]
    rotation = jax.random.randint(jax.random.fold_in(own, 2), (rows, 1), 0, top)
    return jnp.take_along_axis(listing, (jnp.arange(top)[None, :] + rotation) % top, axis=1)


def shares(count, total, bound, skew, full):
    portions = [(1 << 20) // math.isqrt(rank ** skew) + 1 for rank in range(1, count + 1)]
    largest = bound if full else min(bound, max(-(-total // count), total * portions[0] // sum(portions)))
    least = 1 if total - largest >= count - 1 else 0
    given, surplus = [largest] + [least] * (count - 1), total - largest - least * (count - 1)
    while surplus > 0:
        free = [i for i in range(1, count) if given[i] < largest] or [i for i in range(1, count) if given[i] < bound]
        whole, left = sum([portions[i] for i in free]), surplus
        for i in free:
            addition = min(bound - given[i], max(1, left * portions[i] // whole), surplus)
            given[i] = given[i] + addition
            surplus = surplus - addition
    return np.array(given)


def setup_inputs(seed: int = 0) -> dict:
    splits = jax.random.split(jax.random.key(seed), 6)
    images = draw_images(jax.random.fold_in(splits[5], 71), 0)
    bucket_keys = jax.random.split(jax.random.fold_in(splits[1], 1), PARTS_SIZE // P_DEV)
    bucket_turns = jax.random.permutation(jax.random.fold_in(splits[1], 3), PARTS_SIZE // P_DEV)
    bucket = jax.vmap(lambda own, number: assign_block(jax.random.fold_in(splits[1], 2), own, number, P_DEV, N_ORIENT, 1, CAP, 2))(bucket_keys, bucket_turns).reshape((PARTS_SIZE, 1))
    panels = draw_panels(jax.random.fold_in(splits[5], 71), 0)
    tile_slab = draw_tile_slab(jax.random.fold_in(splits[5], 71), 0)
    tile_row = with_ends(jax.random.randint(splits[4], (N_ORIENT, TILES), 0, SLAB_ROWS - G + 1), jax.random.fold_in(splits[4], 1), 0, SLAB_ROWS - G).astype(jnp.int32)
    return dict(images=images, bucket=bucket, panels=panels, tile_slab=tile_slab, tile_row=tile_row)


BETA = 2.0

def slot_table(labels, groups, capacity):
    total_rows = labels.shape[0]
    onehot = (labels[:, None] == jnp.arange(groups, dtype=jnp.int32)[None, :]).astype(jnp.int32)
    ordinal = lax.optimization_barrier(jnp.sum((jnp.cumsum(onehot, axis=0) - 1) * onehot, axis=1))
    matches = onehot[:, :, None] * (ordinal[:, None, None] == jnp.arange(capacity, dtype=jnp.int32)[None, None, :]).astype(jnp.int32)
    sources = lax.optimization_barrier(jnp.sum(matches * jnp.arange(total_rows, dtype=jnp.int32)[:, None, None], axis=0))
    filled = lax.optimization_barrier(jnp.sum(matches, axis=0))
    return (sources, filled, matches)

def reference(images, bucket, panels, tile_slab, tile_row):
    capacity = 2 * P_DEV // N_ORIENT
    device_images = images.reshape(N_ORIENT, N_SLAB, P_DEV, W)
    labels = bucket.reshape(N_ORIENT, N_SLAB, P_DEV)
    sources, filled, matches = jax.vmap(jax.vmap(lambda labels_row: slot_table(labels_row, N_ORIENT, capacity)))(labels)
    within = jnp.arange(ORI, dtype=jnp.int32) % G

    def visit(carry, pair_index):
        volume, loglik = carry
        slab_index = pair_index // N_ORIENT
        bucket_index = pair_index % N_ORIENT
        chosen = sources[:, slab_index, bucket_index]
        alive_slots = filled[:, slab_index, bucket_index]
        rows_of = device_images[:, slab_index]
        gathered = jax.vmap(lambda block_rows, picks: block_rows[picks])(rows_of, chosen)
        gathered = jnp.where(alive_slots[:, :, None] > 0, gathered, jnp.zeros((), gathered.dtype))
        flattened = gathered.reshape(N_ORIENT * capacity, W)
        panel_rows = panels[bucket_index]
        scores = jnp.dot(flattened.astype(jnp.float32), panel_rows.astype(jnp.float32).T) * (BETA / math.sqrt(W))
        largest = lax.optimization_barrier(jnp.max(scores, axis=1, keepdims=True))
        exponent = jnp.exp(scores - largest)
        totals = lax.optimization_barrier(jnp.sum(exponent, axis=1, keepdims=True))
        weights = (exponent / totals).astype(jnp.bfloat16)
        logsum = (largest + jnp.log(totals))[:, 0]
        partial_value = jnp.dot(weights.astype(jnp.float32).T, flattened.astype(jnp.float32)).astype(jnp.bfloat16)
        slabs_of = jnp.repeat(tile_slab[bucket_index], G)
        starts = jnp.repeat(tile_row[bucket_index], G)
        targets = slabs_of * SLAB_ROWS + starts + within
        volume = volume.at[targets].add(partial_value.astype(jnp.float32))
        owners = (jnp.arange(N_ORIENT, dtype=jnp.int32)[:, None] * N_SLAB + slab_index) * P_DEV + chosen
        loglik = loglik.at[owners.reshape(-1)].add(jnp.where(alive_slots.reshape(-1) > 0, logsum, jnp.zeros((), logsum.dtype)))
        return ((volume, loglik), None)
    start = (jnp.zeros((VROWS, W), jnp.float32), jnp.zeros((PARTS_SIZE,), jnp.float32))
    (volume, loglik), _ = lax.scan(visit, start, jnp.arange(N_SLAB * N_ORIENT, dtype=jnp.int32))
    return (volume, loglik)
```

```python
import math

import jax
import jax.numpy as jnp
from jax import lax
from jax.sharding import PartitionSpec as P

G = 8
SLAB_ROWS = 256
BETA = 2.0
CHUNKS = 4


def slots(labels, groups, capacity):
    onehot = (labels[:, None] == jnp.arange(groups, dtype=jnp.int32)[None, :]).astype(jnp.int32)
    ordinal = jnp.sum((jnp.cumsum(onehot, axis=0) - 1) * onehot, axis=1)
    return labels * capacity + ordinal


def body(images, bucket, panels, tile_slab, tile_row):
    orient_count = lax.axis_size("orient")
    slab_count = lax.axis_size("slab")
    per_device, window = images.shape
    capacity = 2 * per_device // orient_count
    slot_total = orient_count * capacity
    panel = panels[0]
    orient_total = panel.shape[0]
    score_scale = BETA / math.sqrt(window)
    owned = window // orient_count
    piece = owned // CHUNKS
    width = window // CHUNKS

    slot_of = slots(bucket[:, 0], orient_count, capacity)
    place = (slot_of[None, :] == jnp.arange(slot_total, dtype=jnp.int32)[:, None])
    select = place.astype(jnp.bfloat16)

    scores = jnp.zeros((slot_total, orient_total), jnp.float32)
    arrived = []
    for j in range(CHUNKS):
        cols = slice(j * width, (j + 1) * width)
        outgoing = jnp.dot(select, images[:, cols], preferred_element_type=jnp.float32)
        outgoing = outgoing.astype(jnp.bfloat16).reshape(orient_count, capacity, width)
        got = lax.all_to_all(outgoing, "orient", split_axis=0, concat_axis=0, tiled=True)
        got = got.reshape(slot_total, width)
        arrived.append(got)
        scores = scores + lax.dot_general(
            got, panel[:, cols], (((1,), (1,)), ((), ())), preferred_element_type=jnp.float32
        )
    scores = scores * score_scale
    largest = jnp.max(scores, axis=1, keepdims=True)
    exponent = jnp.exp(scores - largest)
    totals = jnp.sum(exponent, axis=1, keepdims=True)
    weights = (exponent / totals).astype(jnp.bfloat16)
    logsum = (largest + jnp.log(totals)).reshape(orient_count, capacity)

    within = jnp.arange(G, dtype=jnp.int32)
    rows_total = slab_count * SLAB_ROWS
    targets = (tile_slab * SLAB_ROWS + tile_row)[:, :, None] + within
    targets = targets.reshape(-1)
    spread = (targets[None, :] == jnp.arange(rows_total, dtype=jnp.int32)[:, None]).astype(jnp.bfloat16)

    out = []
    for j in range(CHUNKS):
        parts = []
        for c in range(orient_count):
            begin = c * owned + j * piece
            block = arrived[begin // width][:, begin % width : begin % width + piece]
            parts.append(
                lax.dot_general(
                    weights, block, (((0,), (0,)), ((), ())), preferred_element_type=jnp.float32
                ).astype(jnp.bfloat16)
            )
        partial = jnp.stack(parts)
        landed = lax.all_to_all(partial, "orient", split_axis=0, concat_axis=0, tiled=True)
        landed = landed.reshape(orient_count * orient_total, piece)
        summed = jnp.dot(spread, landed, preferred_element_type=jnp.float32).astype(jnp.bfloat16)
        summed = summed.reshape(slab_count, SLAB_ROWS, piece)
        mine = lax.all_to_all(summed, "slab", split_axis=0, concat_axis=0, tiled=True)
        out.append(jnp.sum(mine, axis=0, dtype=jnp.float32))
    volume = jnp.concatenate(out, axis=1)

    returned = lax.all_to_all(logsum, "orient", split_axis=0, concat_axis=0, tiled=True)
    flat = returned.reshape(-1)
    loglik = jnp.sum(jnp.where(place, flat[:, None], 0.0), axis=0)
    return (volume, loglik)


def solution(mesh):
    in_specs = (
        P(("orient", "slab"), None),
        P(("orient", "slab"), None),
        P("orient", None, None),
        P(),
        P(),
    )
    out_specs = (P("slab", "orient"), P(("orient", "slab")))
    return jax.shard_map(body, mesh=mesh, in_specs=in_specs, out_specs=out_specs, check_vma=False)
```

```python
import functools
import math

import jax
import jax.numpy as jnp
from jax import lax
from jax.experimental import pallas as pl
from jax.experimental.pallas import tpu as pltpu
from jax.sharding import PartitionSpec as P

G = 8
SLAB_ROWS = 256
BETA = 2.0
F32 = jnp.float32
BF16 = jnp.bfloat16
VMEM_LIMIT = 48 * 1024 * 1024


def slots(labels, groups, capacity):
    onehot = (labels[:, None] == jnp.arange(groups, dtype=jnp.int32)[None, :]).astype(jnp.int32)
    ordinal = jnp.sum((jnp.cumsum(onehot, axis=0) - 1) * onehot, axis=1)
    return labels * capacity + ordinal


def swap(x, axis, offset):
    count = lax.axis_size(axis)
    return lax.ppermute(x, axis, [(i, i ^ offset) for i in range(count)])


def call(kernel, name, grid, in_specs, out_specs, out_shape, scratch, flops, size):
    return pl.pallas_call(
        kernel,
        name=name,
        grid_spec=pltpu.PrefetchScalarGridSpec(
            num_scalar_prefetch=1,
            grid=grid,
            in_specs=in_specs,
            out_specs=out_specs,
            scratch_shapes=scratch,
        ),
        out_shape=out_shape,
        compiler_params=pltpu.CompilerParams(vmem_limit_bytes=VMEM_LIMIT),
        cost_estimate=pl.CostEstimate(flops=flops, bytes_accessed=size, transcendentals=0),
    )


def gather_kernel(offsets, capacity, owned, me_ref, slot_ref, images_ref, *rest):
    outs, select = rest[:-1], rest[-1]
    me = me_ref[0]

    @pl.when(pl.program_id(0) == 0)
    def _():
        row = lax.broadcasted_iota(jnp.int32, (capacity, slot_ref.shape[1]), 0)
        for n, offset in enumerate(offsets):
            hit = slot_ref[...] == row + (me ^ offset) * capacity
            select[n * capacity : (n + 1) * capacity, :] = hit.astype(BF16)

    for parity in range(2):
        members = [n for n, offset in enumerate(offsets) if offset & 1 == parity]
        if not members:
            continue
        rows = slice(members[0] * capacity, (members[-1] + 1) * capacity)
        for part in range(2):
            which = (me & 1) ^ parity ^ part
            block = images_ref[:, pl.ds(pl.multiple_of(which * owned, owned), owned)]
            found = jnp.dot(select[rows, :], block, preferred_element_type=F32).astype(BF16)
            for n in members:
                k = n - members[0]
                outs[2 * n + part][...] = found[k * capacity : (k + 1) * capacity]


def gather(offsets, me, slot_of, images, orient_count, capacity):
    offsets = sorted(offsets, key=lambda r: (r & 1, r))
    rows, window = images.shape
    owned = window // orient_count
    blocks = orient_count // 2
    shape = jax.ShapeDtypeStruct((capacity, window // 2), BF16)
    outs = call(
        functools.partial(gather_kernel, offsets, capacity, owned),
        "gather",
        (blocks,),
        [
            pl.BlockSpec((1, rows), lambda j, me: (0, 0)),
            pl.BlockSpec((rows, 2 * owned), lambda j, me: (0, j)),
        ],
        [pl.BlockSpec((capacity, owned), lambda j, me: (0, j))] * (2 * len(offsets)),
        [shape] * (2 * len(offsets)),
        [pltpu.VMEM((len(offsets) * capacity, rows), BF16)],
        2 * len(offsets) * capacity * rows * window,
        2 * window * (rows + len(offsets) * capacity),
    )(me, slot_of, images)
    return {(r, part): outs[2 * n + part] for n, r in enumerate(offsets) for part in range(2)}


def score_kernel(count, owned, scale, me_ref, panel_ref, *rest):
    rows, (weight_ref, logsum_ref, total) = rest[: 2 * count], rest[2 * count :]
    step = pl.program_id(0)
    low = me_ref[0] & 1
    found = None
    for part in range(2):
        block = jnp.concatenate([rows[2 * n + part][...] for n in range(count)], axis=0)
        which = low ^ part
        panel = panel_ref[:, pl.ds(pl.multiple_of(which * owned, owned), owned)]
        term = lax.dot_general(
            block, panel, (((1,), (1,)), ((), ())), preferred_element_type=F32
        )
        found = term if found is None else found + term

    @pl.when(step == 0)
    def _():
        total[...] = found

    @pl.when(step > 0)
    def _():
        total[...] += found

    @pl.when(step == pl.num_programs(0) - 1)
    def _():
        scores = total[...] * scale
        largest = jnp.max(scores, axis=1, keepdims=True)
        exponent = jnp.exp(scores - largest)
        totals = jnp.sum(exponent, axis=1, keepdims=True)
        weight_ref[...] = (exponent / totals).astype(BF16)
        logsum_ref[...] = largest + jnp.log(totals)


def score(me, panel, rows, orient_count, scale):
    count = len(rows) // 2
    orient_total, window = panel.shape
    owned = window // orient_count
    capacity = rows[0].shape[0]
    return call(
        functools.partial(score_kernel, count, owned, scale),
        "score",
        (orient_count // 2,),
        [pl.BlockSpec((orient_total, 2 * owned), lambda j, me: (0, j))]
        + [pl.BlockSpec((capacity, owned), lambda j, me: (0, j))] * len(rows),
        [
            pl.BlockSpec((count * capacity, orient_total), lambda j, me: (0, 0)),
            pl.BlockSpec((count * capacity, 1), lambda j, me: (0, 0)),
        ],
        [
            jax.ShapeDtypeStruct((count * capacity, orient_total), BF16),
            jax.ShapeDtypeStruct((count * capacity, 1), F32),
        ],
        [pltpu.VMEM((count * capacity, orient_total), F32)],
        2 * count * capacity * orient_total * window,
        2 * window * (orient_total + count * capacity),
    )(me, panel, *rows)


def mix_block(mix, rows, stacked):
    begin = 0
    for ref in rows:
        stacked[begin : begin + ref.shape[0], :] = ref[...]
        begin += ref.shape[0]
    return jnp.dot(mix, stacked[...], preferred_element_type=F32)


def send_kernel(groups, count, me_ref, wanted_ref, target_ref, *rest):
    weights, rows = rest[:groups], rest[groups : groups + count]
    out_ref, mix_ref, stacked, joined = rest[groups + count :]

    @pl.when(pl.program_id(0) == 0)
    def _():
        begin = 0
        for ref in weights:
            joined[begin : begin + ref.shape[0], :] = ref[...]
            begin += ref.shape[0]
        spread = (wanted_ref[...] == target_ref[...]).astype(BF16)
        mix_ref[...] = lax.dot_general(
            spread, joined[...], (((1,), (1,)), ((), ())), preferred_element_type=F32
        ).astype(BF16)

    out_ref[...] = mix_block(mix_ref[...], rows, stacked).astype(out_ref.dtype)


def mix_send(me, wanted, target, weights, rows, orient_count):
    volume_rows = wanted.shape[0]
    orient_total = target.shape[1]
    particles = sum(w.shape[0] for w in weights)
    half = rows[0].shape[1]
    blocks = orient_count // 2
    owned = half // blocks
    return call(
        functools.partial(send_kernel, len(weights), len(rows)),
        "mix_send",
        (blocks,),
        [
            pl.BlockSpec((volume_rows, 1), lambda j, me: (0, 0)),
            pl.BlockSpec((1, orient_total), lambda j, me: (0, 0)),
        ]
        + [pl.BlockSpec(w.shape, lambda j, me: (0, 0)) for w in weights]
        + [pl.BlockSpec((r.shape[0], owned), lambda j, me: (0, (me[0] >> 1) ^ j)) for r in rows],
        [
            pl.BlockSpec((volume_rows, owned), lambda j, me: (0, j)),
            pl.BlockSpec((volume_rows, particles), lambda j, me: (0, 0)),
        ],
        [
            jax.ShapeDtypeStruct((volume_rows, half), BF16),
            jax.ShapeDtypeStruct((volume_rows, particles), BF16),
        ],
        [pltpu.VMEM((particles, owned), BF16), pltpu.VMEM((particles, orient_total), BF16)],
        2 * volume_rows * particles * half,
        2 * half * (particles + volume_rows),
    )(me, wanted, target, *weights, *rows)


def keep_kernel(count, blocks, me_ref, mix_ref, got_ref, *rest):
    rows = rest[:count]
    upper_sent, upper_kept, lower_sent, lower_kept, stacked = rest[count:]
    step = pl.program_id(0)
    total = mix_block(mix_ref[...], rows, stacked) + got_ref[...].astype(F32)
    middle = total.shape[0] // 2
    upper, lower = total[:middle], total[middle:]

    @pl.when(step % 2 == 1)
    def _():
        upper_sent[step // 2] = upper.astype(BF16)

    @pl.when(step % 2 == 0)
    def _():
        upper_kept[step // 2] = upper

    @pl.when(step >= blocks // 2)
    def _():
        lower_sent[step % (blocks // 2)] = lower.astype(BF16)

    @pl.when(step < blocks // 2)
    def _():
        lower_kept[step % (blocks // 2)] = lower


def mix_keep(me, mix, first_row, got, rows, orient_count):
    particles = mix.shape[1]
    half = rows[0].shape[1]
    blocks = orient_count // 2
    owned = half // blocks
    place = first_row // SLAB_ROWS
    part = (blocks // 2, SLAB_ROWS // 2, owned)
    return call(
        functools.partial(keep_kernel, len(rows), blocks),
        "mix_keep",
        (blocks,),
        [
            pl.BlockSpec((SLAB_ROWS, particles), lambda j, me: (place, 0)),
            pl.BlockSpec((SLAB_ROWS, owned), lambda j, me: (place, j)),
        ]
        + [pl.BlockSpec((r.shape[0], owned), lambda j, me: (0, (me[0] >> 1) ^ j)) for r in rows],
        [pl.BlockSpec(part, lambda j, me: (0, 0, 0))] * 4,
        [jax.ShapeDtypeStruct(part, BF16), jax.ShapeDtypeStruct(part, F32)] * 2,
        [pltpu.VMEM((particles, owned), BF16)],
        2 * SLAB_ROWS * particles * half,
        2 * half * (particles + 2 * SLAB_ROWS),
    )(me, mix, got, *rows)


def reduce_chips(upper_sent, upper_kept, lower_sent, lower_kept, orient_count):
    bits = list(range(1, orient_count.bit_length() - 1))
    for n in range(len(bits)):
        upper = upper_kept + swap(upper_sent, "orient", 1 << bits[n]).astype(F32)
        lower = lower_kept + swap(lower_sent, "orient", 1 << bits[-1 - n]).astype(F32)
        left = upper.shape[0]
        upper_kept, upper_sent = upper[0::2], upper[1::2].astype(BF16)
        lower_kept, lower_sent = lower[: (left + 1) // 2], lower[(left + 1) // 2 :].astype(BF16)
    return jnp.concatenate([upper_kept[0], lower_kept[0]])


def body(images, bucket, panels, tile_slab, tile_row):
    orient_count = lax.axis_size("orient")
    slab_count = lax.axis_size("slab")
    me = lax.axis_index("orient")
    here = lax.axis_index("slab")
    me_ref = me.astype(jnp.int32).reshape(1)
    per_device, window = images.shape
    capacity = 2 * per_device // orient_count
    panel = panels[0]
    score_scale = BETA / math.sqrt(window)

    slot_of = slots(bucket[:, 0], orient_count, capacity)
    slot_row = slot_of[None, :]

    far = sorted(range(2, orient_count), key=lambda r: (-(r >> 1).bit_count(), r & 1, r))
    outgoing = gather(far[:2], me_ref, slot_row, images, orient_count, capacity)
    outgoing |= gather([0, 1] + far[2:], me_ref, slot_row, images, orient_count, capacity)
    arrived = {(0, part): outgoing[0, part] for part in range(2)}
    for offset in far[:2] + [1] + far[2:]:
        for part in range(2):
            arrived[offset, part] = swap(outgoing[offset, part], "orient", offset)

    order = [0, 1] + far
    weights, logsums = [], []
    for first in range(0, orient_count, 2):
        rows = [arrived[r, part] for r in order[first : first + 2] for part in range(2)]
        weight, logsum = score(me_ref, panel, rows, orient_count, score_scale)
        weights.append(weight)
        logsums.append(logsum.reshape(2, capacity))

    my_slab = lax.dynamic_index_in_dim(tile_slab, me, 0, keepdims=False)
    my_row = lax.dynamic_index_in_dim(tile_row, me, 0, keepdims=False)
    within = jnp.arange(G, dtype=jnp.int32)
    target = (my_slab[:, None] * SLAB_ROWS + my_row[:, None] + within).reshape(1, -1)
    slab_order = [2, 3, 1, 0] if slab_count == 4 else list(range(slab_count - 1, -1, -1))
    ours = [arrived[r, 0] for r in order]
    theirs = [arrived[r, 1] for r in order]
    volume = None
    incoming = []
    for lot in (slab_order[:1], slab_order[1:]):
        wanted = jnp.concatenate(
            [(here ^ r) * SLAB_ROWS + jnp.arange(SLAB_ROWS, dtype=jnp.int32) for r in lot]
        )
        sent, mix = mix_send(me_ref, wanted[:, None], target, weights, theirs, orient_count)
        got = swap(sent, "orient", 1)
        for n, offset in enumerate(lot):
            split = mix_keep(me_ref, mix, n * SLAB_ROWS, got, ours, orient_count)
            total = reduce_chips(*split, orient_count)
            if offset:
                incoming.append(swap(total.astype(BF16), "slab", offset))
            else:
                volume = total
    for block in incoming:
        volume = volume + block.astype(F32)

    logsum = jnp.concatenate(logsums)
    logsum = jnp.stack([logsum[order.index(r)] for r in range(orient_count)])
    logsum = jnp.take(logsum, me ^ jnp.arange(orient_count, dtype=jnp.int32), axis=0)
    returned = lax.all_to_all(logsum[:, None, :], "orient", split_axis=0, concat_axis=0, tiled=True)
    place = slot_of[None, :] == jnp.arange(orient_count * capacity, dtype=jnp.int32)[:, None]
    loglik = jnp.sum(jnp.where(place, returned.reshape(-1)[:, None], 0.0), axis=0)
    return (volume, loglik)


def solution(mesh):
    in_specs = (
        P(("orient", "slab"), None),
        P(("orient", "slab"), None),
        P("orient", None, None),
        P(),
        P(),
    )
    out_specs = (P("slab", "orient"), P(("orient", "slab")))
    return jax.shard_map(body, mesh=mesh, in_specs=in_specs, out_specs=out_specs, check_vma=False)
```

```python
import functools
import math

import jax
import jax.numpy as jnp
from jax import lax
from jax.experimental import pallas as pl
from jax.experimental.pallas import tpu as pltpu
from jax.sharding import PartitionSpec as P

G = 8
SLAB_ROWS = 256
BETA = 2.0
F32 = jnp.float32
BF16 = jnp.bfloat16
VMEM_LIMIT = 16 * 1024 * 1024


def slots(labels, groups, capacity):
    onehot = (labels[:, None] == jnp.arange(groups, dtype=jnp.int32)[None, :]).astype(jnp.int32)
    ordinal = jnp.sum((jnp.cumsum(onehot, axis=0) - 1) * onehot, axis=1)
    return labels * capacity + ordinal


def after(x, token):
    return lax.optimization_barrier((x, token))[0]


def swap(x, axis, offset):
    count = lax.axis_size(axis)
    return lax.ppermute(x, axis, [(i, i ^ offset) for i in range(count)])


def call(kernel, name, grid, in_specs, out_specs, out_shape, scratch, flops, size):
    return pl.pallas_call(
        kernel,
        name=name,
        grid_spec=pltpu.PrefetchScalarGridSpec(
            num_scalar_prefetch=1,
            grid=grid,
            in_specs=in_specs,
            out_specs=out_specs,
            scratch_shapes=scratch,
        ),
        out_shape=out_shape,
        compiler_params=pltpu.CompilerParams(vmem_limit_bytes=VMEM_LIMIT),
        cost_estimate=pl.CostEstimate(flops=20 * flops, bytes_accessed=20 * size, transcendentals=0),
    )


def gather_kernel(chips, capacity, owned, me_ref, slot_ref, images_ref, *rest):
    outs, select = rest[:-1], rest[-1]
    low, chip = me_ref[0] & 1, me_ref[0] >> 1
    both = 2 * capacity

    @pl.when(pl.program_id(0) == 0)
    def _():
        row = lax.broadcasted_iota(jnp.int32, (both, slot_ref.shape[1]), 0)
        for n, offset in enumerate(chips):
            hit = slot_ref[...] == row + (chip ^ offset) * both
            select[n * both : (n + 1) * both, :] = hit.astype(BF16)

    for which in range(2):
        block = images_ref[:, which * owned : (which + 1) * owned]
        found = jnp.dot(select[...], block, preferred_element_type=F32).astype(BF16)
        for core in range(2):

            @pl.when(low == core)
            def _():
                for n in range(len(chips)):
                    for member in range(2):
                        begin = n * both + member * capacity
                        rows = found[begin : begin + capacity]
                        out = 2 * n + (which ^ core)
                        outs[2 * out + member][...] = rows


def gather(chips, me, slot_of, images, orient_count, capacity):
    rows, window = images.shape
    owned = window // orient_count
    count = 4 * len(chips)
    outs = call(
        functools.partial(gather_kernel, chips, capacity, owned),
        "gather",
        (orient_count // 2,),
        [
            pl.BlockSpec((1, rows), lambda j, me: (0, 0)),
            pl.BlockSpec((rows, 2 * owned), lambda j, me: (0, j)),
        ],
        [pl.BlockSpec((capacity, owned), lambda j, me: (0, j))] * count,
        [jax.ShapeDtypeStruct((capacity, window // 2), BF16)] * count,
        [pltpu.VMEM((2 * len(chips) * capacity, rows), BF16)],
        4 * len(chips) * capacity * rows * window,
        2 * window * (rows + 2 * len(chips) * capacity),
    )(me, slot_of, images)
    offsets = [2 * q + swapped for q in chips for swapped in range(2)]
    return {r: [outs[2 * n], outs[2 * n + 1]] for n, r in enumerate(offsets)}


def score_kernel(members, count, me_ref, panels_ref, *rest):
    rows, out_ref = rest[:-1], rest[-1]
    for n, member in enumerate(members):
        block = jnp.concatenate([ref[...] for ref in rows[n * count : (n + 1) * count]], axis=0)
        term = lax.dot_general(
            block, panels_ref[n], (((1,), (1,)), ((), ())), preferred_element_type=F32
        )

        @pl.when(pl.program_id(0) == 0)
        def _():
            out_ref[n] = term

        @pl.when(pl.program_id(0) > 0)
        def _():
            out_ref[n] += term


def score(members, me, panels, pieces, orient_count):
    rows = [piece[member] for member in members for piece in pieces]
    _, orient_total, window = panels.shape
    owned = window // orient_count
    capacity = rows[0].shape[0]
    lead = members[0]
    shape = (len(members), len(pieces) * capacity, orient_total)
    return call(
        functools.partial(score_kernel, members, len(pieces)),
        "score",
        (orient_count // 2,),
        [
            pl.BlockSpec(
                (len(members), orient_total, owned), lambda j, me: (lead, 0, 2 * j + (me[0] & 1))
            )
        ]
        + [pl.BlockSpec((capacity, owned), lambda j, me: (0, j))] * len(rows),
        pl.BlockSpec(shape, lambda j, me: (0, 0, 0)),
        jax.ShapeDtypeStruct(shape, F32),
        [],
        shape[0] * shape[1] * orient_total * window,
        2 * window * (orient_total + shape[1]),
    )(me, panels, *rows)


def softmax(mine, got, capacity, scale):
    count = got.shape[0] // capacity
    got = jnp.concatenate(
        [got[(n ^ 1) * capacity : ((n ^ 1) + 1) * capacity] for n in range(count)], axis=0
    )
    scores = (mine + got) * scale
    largest = jnp.max(scores, axis=1, keepdims=True)
    exponent = jnp.exp(scores - largest)
    totals = jnp.sum(exponent, axis=1, keepdims=True)
    return (exponent / totals).astype(BF16), largest + jnp.log(totals)


def weigh_kernel(capacity, scale, me_ref, mine_ref, got_ref, weight_ref, logsum_ref):
    weight_ref[0], logsum_ref[0] = softmax(mine_ref[0], got_ref[0], capacity, scale)


def weigh(me, mine, got, capacity, scale):
    members, rows, orient_total = mine.shape
    block = pl.BlockSpec((1, rows, orient_total), lambda j, me: (j, 0, 0))
    return call(
        functools.partial(weigh_kernel, capacity, scale),
        "weigh",
        (members,),
        [block, block],
        [block, pl.BlockSpec((1, rows, 1), lambda j, me: (j, 0, 0))],
        [
            jax.ShapeDtypeStruct(mine.shape, BF16),
            jax.ShapeDtypeStruct((members, rows, 1), F32),
        ],
        [],
        10 * members * rows * orient_total,
        10 * members * rows * orient_total,
    )(me, mine, got)


def matrix_kernel(capacity, scale, me_ref, wanted_ref, target_ref, early_ref, *rest):
    mine, got, (logsum_ref, mix_ref, joined) = rest[:2], rest[2:4], rest[4:]
    early = early_ref.shape[1]
    late = mine[0].shape[1]
    for member in range(2):
        joined[:early, :] = early_ref[member]
        joined[early:, :], logsum_ref[member] = softmax(
            mine[member][0], got[member][0], capacity, scale
        )
        weights = joined[...]
        for n in range(wanted_ref.shape[0] // SLAB_ROWS):
            rows = slice(n * SLAB_ROWS, (n + 1) * SLAB_ROWS)
            spread = (wanted_ref[rows, :] == target_ref[member : member + 1, :]).astype(BF16)
            mix_ref[rows, member * (early + late) : (member + 1) * (early + late)] = lax.dot_general(
                spread, weights, (((1,), (1,)), ((), ())), preferred_element_type=F32
            ).astype(BF16)


def matrix(me, wanted, target, early, mine, got, capacity, scale):
    volume_rows = wanted.shape[0]
    _, late, orient_total = mine[0].shape
    particles = early.shape[1] + late

    def whole(shape):
        return pl.BlockSpec(shape, lambda j, me: (0,) * len(shape))

    return call(
        functools.partial(matrix_kernel, capacity, scale),
        "matrix",
        (1,),
        [whole(x.shape) for x in (wanted, target, early, *mine, *got)],
        [whole((2, late, 1)), whole((volume_rows, 2 * particles))],
        [
            jax.ShapeDtypeStruct((2, late, 1), F32),
            jax.ShapeDtypeStruct((volume_rows, 2 * particles), BF16),
        ],
        [pltpu.VMEM((particles, orient_total), BF16)],
        4 * volume_rows * particles * orient_total,
        4 * volume_rows * particles,
    )(me, wanted, target, early, *mine, *got)


def mix_kernel(count, blocks, me_ref, mix_ref, *rest):
    rows = rest[:count]
    upper_sent, upper_kept, lower_sent, lower_kept, stacked = rest[count:]
    step = pl.program_id(0)
    begin = 0
    for ref in rows:
        stacked[begin : begin + ref.shape[0], :] = ref[...]
        begin += ref.shape[0]
    total = jnp.dot(mix_ref[...], stacked[...], preferred_element_type=F32)
    middle = SLAB_ROWS // 2
    parts = [total[begin : begin + middle] for begin in range(0, total.shape[0], middle)]
    upper = jnp.concatenate(parts[0::2], axis=0)
    lower = jnp.concatenate(parts[1::2], axis=0)

    @pl.when(step % 2 == 1)
    def _():
        upper_sent[step // 2] = upper.astype(BF16)

    @pl.when(step % 2 == 0)
    def _():
        upper_kept[step // 2] = upper

    @pl.when(step >= blocks // 2)
    def _():
        lower_sent[step % (blocks // 2)] = lower.astype(BF16)

    @pl.when(step < blocks // 2)
    def _():
        lower_kept[step % (blocks // 2)] = lower


def mix(me, matrix, place, pieces, orient_count):
    rows = [piece[member] for member in range(2) for piece in pieces]
    particles = matrix.shape[1]
    half = rows[0].shape[1]
    blocks = orient_count // 2
    owned = half // blocks
    volume_rows = 2 * SLAB_ROWS
    part = (blocks // 2, SLAB_ROWS, owned)
    return call(
        functools.partial(mix_kernel, len(rows), blocks),
        "mix",
        (blocks,),
        [pl.BlockSpec((volume_rows, particles), lambda j, me: (place, 0))]
        + [pl.BlockSpec((r.shape[0], owned), lambda j, me: (0, (me[0] >> 1) ^ j)) for r in rows],
        [pl.BlockSpec(part, lambda j, me: (0, 0, 0))] * 4,
        [jax.ShapeDtypeStruct(part, BF16), jax.ShapeDtypeStruct(part, F32)] * 2,
        [pltpu.VMEM((particles, owned), BF16)],
        2 * volume_rows * particles * half,
        2 * half * (particles + volume_rows),
    )(me, matrix, *rows)


def exchange(state, n, bits):
    upper_sent, upper_kept, lower_sent, lower_kept = state
    got = (
        swap(upper_sent, "orient", 1 << bits[n]),
        swap(lower_sent, "orient", 1 << bits[-1 - n]),
    )
    return got, upper_kept, lower_kept


def add_split(got, upper_kept, lower_kept):
    upper = upper_kept + got[0].astype(F32)
    lower = lower_kept + got[1].astype(F32)
    middle = (lower.shape[0] + 1) // 2
    return upper[1::2].astype(BF16), upper[0::2], lower[middle:].astype(BF16), lower[:middle]


def body(images, bucket, panels, tile_slab, tile_row):
    orient_count = lax.axis_size("orient")
    slab_count = lax.axis_size("slab")
    me = lax.axis_index("orient")
    here = lax.axis_index("slab")
    me_ref = me.astype(jnp.int32).reshape(1)
    per_device, window = images.shape
    capacity = 2 * per_device // orient_count
    panel = panels[0]
    score_scale = BETA / math.sqrt(window)

    slot_of = slots(bucket[:, 0], orient_count, capacity)
    slot_row = slot_of[None, :]

    chips = sorted(range(1, orient_count // 2), key=lambda q: (-q.bit_count(), q))
    far, near = chips[:-2], chips[-2:]
    outgoing = gather(far[:1], me_ref, slot_row, images, orient_count, capacity)
    early = [0, 1] + [2 * q + swapped for q in far for swapped in range(2)]
    late = [2 * q + swapped for q in near for swapped in range(2)]
    order = early + late
    arrived = {}
    for offset in early[2:4]:
        arrived[offset] = [swap(half, "orient", offset) for half in outgoing[offset]]
    images = after(images, (arrived[early[2]][0], arrived[early[3]][0]))
    outgoing |= gather([0] + chips[1:], me_ref, slot_row, images, orient_count, capacity)
    arrived[0] = outgoing[0]
    for offset in early[4:] + early[1:2] + [2 * q + swapped for swapped in range(2) for q in near]:
        arrived[offset] = [swap(half, "orient", offset) for half in outgoing[offset]]
    pieces = [arrived[r] for r in order]

    both = lax.all_gather(
        panel, "orient", axis_index_groups=[[2 * q, 2 * q + 1] for q in range(orient_count // 2)]
    )
    early_pieces, late_pieces = pieces[: len(early)], pieces[len(early) :]
    early_scores = score((0, 1), me_ref, both, early_pieces, orient_count)
    early_weights, early_logs = weigh(
        me_ref, early_scores, swap(early_scores, "orient", 1), capacity, score_scale
    )
    late_scores, got_late = [], []
    for member in range(2):
        if member == 1:
            both = after(both, early_weights)
        found = score((member,), me_ref, both, late_pieces, orient_count)
        late_scores.append(found)
        got_late.append(swap(found, "orient", 1))

    within = jnp.arange(G, dtype=jnp.int32)
    buckets = (me & ~1) + jnp.arange(2, dtype=jnp.int32)
    first_rows = jnp.take(tile_slab, buckets, axis=0) * SLAB_ROWS + jnp.take(tile_row, buckets, axis=0)
    target = (first_rows[:, :, None] + within).reshape(2, -1)
    slab_order = list(range(slab_count - 1, -1, -1))
    wanted = jnp.concatenate(
        [(here ^ r) * SLAB_ROWS + jnp.arange(SLAB_ROWS, dtype=jnp.int32) for r in slab_order]
    )[:, None]
    late_logs, mixing = matrix(me_ref, wanted, target, early_weights, late_scores, got_late, capacity, score_scale)

    count = slab_count // 2
    bits = list(range(1, orient_count.bit_length() - 1))
    split, stage, sums = {}, {}, {}

    def keep(n, token):
        which = mixing if token is None else after(mixing, token)
        split[n] = mix(me_ref, which, n, pieces, orient_count)
        return split[n][1]

    def begin(n, token):
        state = tuple(split[n])
        if token is not None:
            state = after(state, token)
        stage[n] = exchange(state, 0, bits)

    def advance(n, step, token):
        landed, upper, lower = stage[n]
        state = add_split(after(landed, token), upper, lower)
        stage[n] = exchange(state, step, bits)
        return state[1]

    def gathered(n, token, tie=None):
        for step in range(2, len(bits)):
            token = advance(n, step, token)
        landed, upper, lower = stage[n]
        landed = after(landed, token if tie is None else (token, tie))
        upper = upper[0] + landed[0][0].astype(F32)
        lower = lower[0] + landed[1][0].astype(F32)
        middle = SLAB_ROWS // 2
        return [
            jnp.concatenate([upper[:middle], lower[:middle]]),
            jnp.concatenate([upper[middle:], lower[middle:]]),
        ]

    def deliver(n, totals):
        for total, offset in zip(totals, slab_order[2 * n : 2 * n + 2]):
            for block in sums.get(offset, []):
                total = total + block.astype(F32)
            if offset:
                step = offset & -offset
                token = total.astype(BF16)
                sums.setdefault(offset ^ step, []).append(swap(token, "slab", step))
        return total, token

    token = keep(0, None)
    begin(0, None)
    for n in range(count):
        if n + 1 < count:
            token = keep(n + 1, token)
        landed = stage[n][0]
        token = advance(n, 1, token)
        if n + 1 < count:
            begin(n + 1, landed)
        totals = gathered(n, token, sums[0] if n + 1 == count else None)
        volume, token = deliver(n, totals)
    logs = jnp.concatenate([early_logs, late_logs], axis=1)[:, :, 0]
    logs = lax.dynamic_index_in_dim(logs, me & 1, 0, keepdims=False)
    logsum = after(logs.reshape(orient_count, capacity), token)

    logsum = jnp.stack([logsum[order.index(r)] for r in range(orient_count)])
    logsum = jnp.take(logsum, me ^ jnp.arange(orient_count, dtype=jnp.int32), axis=0)
    returned = lax.all_to_all(logsum[:, None, :], "orient", split_axis=0, concat_axis=0, tiled=True)
    place = slot_of[None, :] == jnp.arange(orient_count * capacity, dtype=jnp.int32)[:, None]
    loglik = jnp.sum(jnp.where(place, returned.reshape(-1)[:, None], 0.0), axis=0)
    return (volume, loglik)


def solution(mesh):
    in_specs = (
        P(("orient", "slab"), None),
        P(("orient", "slab"), None),
        P("orient", None, None),
        P(),
        P(),
    )
    out_specs = (P("slab", "orient"), P(("orient", "slab")))
    return jax.shard_map(body, mesh=mesh, in_specs=in_specs, out_specs=out_specs, check_vma=False)
```

```python
import functools
import math

import jax
import jax.numpy as jnp
from jax import lax
from jax.experimental import pallas as pl
from jax.experimental.pallas import tpu as pltpu
from jax.sharding import PartitionSpec as P

G = 8
SLAB_ROWS = 256
BETA = 2.0
F32 = jnp.float32
BF16 = jnp.bfloat16
VMEM_LIMIT = 16 * 1024 * 1024


def slots(labels, groups, capacity):
    onehot = (labels[:, None] == jnp.arange(groups, dtype=jnp.int32)[None, :]).astype(jnp.int32)
    ordinal = jnp.sum((jnp.cumsum(onehot, axis=0) - 1) * onehot, axis=1)
    return labels * capacity + ordinal


def after(x, token):
    return lax.optimization_barrier((x, token))[0]


def swap(x, axis, offset):
    count = lax.axis_size(axis)
    return lax.ppermute(x, axis, [(i, i ^ offset) for i in range(count)])


def call(kernel, name, grid, in_specs, out_specs, out_shape, scratch, flops, size):
    return pl.pallas_call(
        kernel,
        name=name,
        grid_spec=pltpu.PrefetchScalarGridSpec(
            num_scalar_prefetch=1,
            grid=grid,
            in_specs=in_specs,
            out_specs=out_specs,
            scratch_shapes=scratch,
        ),
        out_shape=out_shape,
        compiler_params=pltpu.CompilerParams(vmem_limit_bytes=VMEM_LIMIT),
        cost_estimate=pl.CostEstimate(flops=20 * flops, bytes_accessed=20 * size, transcendentals=0),
    )


def gather_kernel(chips, capacity, owned, me_ref, slot_ref, images_ref, *rest):
    outs, select = rest[:-1], rest[-1]
    low, chip = me_ref[0] & 1, me_ref[0] >> 1
    both = 2 * capacity

    @pl.when(pl.program_id(0) == 0)
    def _():
        row = lax.broadcasted_iota(jnp.int32, (both, slot_ref.shape[1]), 0)
        for n, offset in enumerate(chips):
            hit = slot_ref[...] == row + (chip ^ offset) * both
            select[n * both : (n + 1) * both, :] = hit.astype(BF16)

    for which in range(2):
        block = images_ref[:, which * owned : (which + 1) * owned]
        found = jnp.dot(select[...], block, preferred_element_type=F32).astype(BF16)
        for core in range(2):

            @pl.when(low == core)
            def _():
                for n in range(len(chips)):
                    for member in range(2):
                        begin = n * both + member * capacity
                        rows = found[begin : begin + capacity]
                        out = 2 * n + (which ^ core)
                        outs[2 * out + member][...] = rows


def gather(chips, me, slot_of, images, orient_count, capacity):
    rows, window = images.shape
    owned = window // orient_count
    count = 4 * len(chips)
    outs = call(
        functools.partial(gather_kernel, chips, capacity, owned),
        "gather",
        (orient_count // 2,),
        [
            pl.BlockSpec((1, rows), lambda j, me: (0, 0)),
            pl.BlockSpec((rows, 2 * owned), lambda j, me: (0, j)),
        ],
        [pl.BlockSpec((capacity, owned), lambda j, me: (0, j))] * count,
        [jax.ShapeDtypeStruct((capacity, window // 2), BF16)] * count,
        [pltpu.VMEM((2 * len(chips) * capacity, rows), BF16)],
        4 * len(chips) * capacity * rows * window,
        2 * window * (rows + 2 * len(chips) * capacity),
    )(me, slot_of, images)
    offsets = [2 * q + swapped for q in chips for swapped in range(2)]
    return {r: [outs[2 * n], outs[2 * n + 1]] for n, r in enumerate(offsets)}


def score_kernel(members, count, me_ref, panels_ref, *rest):
    rows, out_ref = rest[:-1], rest[-1]
    for n, member in enumerate(members):
        block = jnp.concatenate([ref[...] for ref in rows[n * count : (n + 1) * count]], axis=0)
        term = lax.dot_general(
            block, panels_ref[n], (((1,), (1,)), ((), ())), preferred_element_type=F32
        )

        @pl.when(pl.program_id(0) == 0)
        def _():
            out_ref[n] = term

        @pl.when(pl.program_id(0) > 0)
        def _():
            out_ref[n] += term


def score(members, me, panels, pieces, orient_count):
    rows = [piece[member] for member in members for piece in pieces]
    _, orient_total, window = panels.shape
    owned = window // orient_count
    capacity = rows[0].shape[0]
    lead = members[0]
    shape = (len(members), len(pieces) * capacity, orient_total)
    return call(
        functools.partial(score_kernel, members, len(pieces)),
        "score",
        (orient_count // 2,),
        [
            pl.BlockSpec(
                (len(members), orient_total, owned), lambda j, me: (lead, 0, 2 * j + (me[0] & 1))
            )
        ]
        + [pl.BlockSpec((capacity, owned), lambda j, me: (0, j))] * len(rows),
        pl.BlockSpec(shape, lambda j, me: (0, 0, 0)),
        jax.ShapeDtypeStruct(shape, F32),
        [],
        shape[0] * shape[1] * orient_total * window,
        2 * window * (orient_total + shape[1]),
    )(me, panels, *rows)


def softmax(mine, got, capacity, scale):
    count = got.shape[0] // capacity
    got = jnp.concatenate(
        [got[(n ^ 1) * capacity : ((n ^ 1) + 1) * capacity] for n in range(count)], axis=0
    )
    scores = (mine + got) * scale
    largest = jnp.max(scores, axis=1, keepdims=True)
    exponent = jnp.exp(scores - largest)
    totals = jnp.sum(exponent, axis=1, keepdims=True)
    return (exponent / totals).astype(BF16), largest + jnp.log(totals)


def weigh_kernel(capacity, scale, me_ref, mine_ref, got_ref, weight_ref, logsum_ref):
    weight_ref[0], logsum_ref[0] = softmax(mine_ref[0], got_ref[0], capacity, scale)


def weigh(me, mine, got, capacity, scale):
    members, rows, orient_total = mine.shape
    block = pl.BlockSpec((1, rows, orient_total), lambda j, me: (j, 0, 0))
    return call(
        functools.partial(weigh_kernel, capacity, scale),
        "weigh",
        (members,),
        [block, block],
        [block, pl.BlockSpec((1, rows, 1), lambda j, me: (j, 0, 0))],
        [
            jax.ShapeDtypeStruct(mine.shape, BF16),
            jax.ShapeDtypeStruct((members, rows, 1), F32),
        ],
        [],
        10 * members * rows * orient_total,
        10 * members * rows * orient_total,
    )(me, mine, got)


def matrix_kernel(capacity, scale, me_ref, wanted_ref, target_ref, early_ref, *rest):
    mine, got, (logsum_ref, mix_ref, joined) = rest[:2], rest[2:4], rest[4:]
    early = early_ref.shape[1]
    late = mine[0].shape[1]
    for member in range(2):
        joined[:early, :] = early_ref[member]
        joined[early:, :], logsum_ref[member] = softmax(
            mine[member][0], got[member][0], capacity, scale
        )
        weights = joined[...]
        for n in range(wanted_ref.shape[0] // SLAB_ROWS):
            rows = slice(n * SLAB_ROWS, (n + 1) * SLAB_ROWS)
            spread = (wanted_ref[rows, :] == target_ref[member : member + 1, :]).astype(BF16)
            mix_ref[rows, member * (early + late) : (member + 1) * (early + late)] = lax.dot_general(
                spread, weights, (((1,), (1,)), ((), ())), preferred_element_type=F32
            ).astype(BF16)


def matrix(me, wanted, target, early, mine, got, capacity, scale):
    volume_rows = wanted.shape[0]
    _, late, orient_total = mine[0].shape
    particles = early.shape[1] + late

    def whole(shape):
        return pl.BlockSpec(shape, lambda j, me: (0,) * len(shape))

    return call(
        functools.partial(matrix_kernel, capacity, scale),
        "matrix",
        (1,),
        [whole(x.shape) for x in (wanted, target, early, *mine, *got)],
        [whole((2, late, 1)), whole((volume_rows, 2 * particles))],
        [
            jax.ShapeDtypeStruct((2, late, 1), F32),
            jax.ShapeDtypeStruct((volume_rows, 2 * particles), BF16),
        ],
        [pltpu.VMEM((particles, orient_total), BF16)],
        4 * volume_rows * particles * orient_total,
        4 * volume_rows * particles,
    )(me, wanted, target, early, *mine, *got)


def mix_kernel(count, blocks, me_ref, mix_ref, *rest):
    rows = rest[:count]
    upper_sent, upper_kept, lower_sent, lower_kept, stacked = rest[count:]
    step = pl.program_id(0)
    begin = 0
    for ref in rows:
        stacked[begin : begin + ref.shape[0], :] = ref[...]
        begin += ref.shape[0]
    total = jnp.dot(mix_ref[...], stacked[...], preferred_element_type=F32)
    middle = SLAB_ROWS // 2
    parts = [total[begin : begin + middle] for begin in range(0, total.shape[0], middle)]
    upper = jnp.concatenate(parts[0::2], axis=0)
    lower = jnp.concatenate(parts[1::2], axis=0)

    @pl.when(step % 2 == 1)
    def _():
        upper_sent[step // 2] = upper.astype(BF16)

    @pl.when(step % 2 == 0)
    def _():
        upper_kept[step // 2] = upper

    @pl.when(step >= blocks // 2)
    def _():
        lower_sent[step % (blocks // 2)] = lower.astype(BF16)

    @pl.when(step < blocks // 2)
    def _():
        lower_kept[step % (blocks // 2)] = lower


def mix(me, matrix, place, pieces, orient_count):
    rows = [piece[member] for member in range(2) for piece in pieces]
    particles = matrix.shape[1]
    half = rows[0].shape[1]
    blocks = orient_count // 2
    owned = half // blocks
    volume_rows = 2 * SLAB_ROWS
    part = (blocks // 2, SLAB_ROWS, owned)
    return call(
        functools.partial(mix_kernel, len(rows), blocks),
        "mix",
        (blocks,),
        [pl.BlockSpec((volume_rows, particles), lambda j, me: (place, 0))]
        + [pl.BlockSpec((r.shape[0], owned), lambda j, me: (0, (me[0] >> 1) ^ j)) for r in rows],
        [pl.BlockSpec(part, lambda j, me: (0, 0, 0))] * 4,
        [jax.ShapeDtypeStruct(part, BF16), jax.ShapeDtypeStruct(part, F32)] * 2,
        [pltpu.VMEM((particles, owned), BF16)],
        2 * volume_rows * particles * half,
        2 * half * (particles + volume_rows),
    )(me, matrix, *rows)


def exchange(state, n, bits):
    upper_sent, upper_kept, lower_sent, lower_kept = state
    got = (
        swap(upper_sent, "orient", 1 << bits[n]),
        swap(lower_sent, "orient", 1 << bits[-1 - n]),
    )
    return got, upper_kept, lower_kept


def add_split(got, upper_kept, lower_kept):
    upper = upper_kept + got[0].astype(F32)
    lower = lower_kept + got[1].astype(F32)
    middle = (lower.shape[0] + 1) // 2
    return upper[1::2].astype(BF16), upper[0::2], lower[middle:].astype(BF16), lower[:middle]


def body(images, bucket, panels, tile_slab, tile_row):
    orient_count = lax.axis_size("orient")
    slab_count = lax.axis_size("slab")
    me = lax.axis_index("orient")
    here = lax.axis_index("slab")
    me_ref = me.astype(jnp.int32).reshape(1)
    per_device, window = images.shape
    capacity = 2 * per_device // orient_count
    panel = panels[0]
    score_scale = BETA / math.sqrt(window)

    slot_of = slots(bucket[:, 0], orient_count, capacity)
    slot_row = slot_of[None, :]

    chips = sorted(range(1, orient_count // 2), key=lambda q: (-q.bit_count(), q))
    far, near = chips[:-2], chips[-2:]
    outgoing = gather(far[:1], me_ref, slot_row, images, orient_count, capacity)
    early = [0, 1] + [2 * q + swapped for q in far for swapped in range(2)]
    late = [2 * q + swapped for q in near for swapped in range(2)]
    order = early + late
    arrived = {}
    for offset in early[2:4]:
        arrived[offset] = [swap(half, "orient", offset) for half in outgoing[offset]]
    images = after(images, (arrived[early[2]][0], arrived[early[3]][0]))
    outgoing |= gather([0] + chips[1:], me_ref, slot_row, images, orient_count, capacity)
    arrived[0] = outgoing[0]
    for offset in early[4:] + early[1:2] + [2 * q + swapped for swapped in range(2) for q in near]:
        arrived[offset] = [swap(half, "orient", offset) for half in outgoing[offset]]
    pieces = [arrived[r] for r in order]

    both = lax.all_gather(
        panel, "orient", axis_index_groups=[[2 * q, 2 * q + 1] for q in range(orient_count // 2)]
    )
    early_pieces, late_pieces = pieces[: len(early)], pieces[len(early) :]
    early_scores = score((0, 1), me_ref, both, early_pieces, orient_count)
    early_weights, early_logs = weigh(
        me_ref, early_scores, swap(early_scores, "orient", 1), capacity, score_scale
    )
    late_scores, got_late = [], []
    for member in range(2):
        if member == 1:
            both = after(both, early_weights)
        found = score((member,), me_ref, both, late_pieces, orient_count)
        late_scores.append(found)
        got_late.append(swap(found, "orient", 1))

    within = jnp.arange(G, dtype=jnp.int32)
    buckets = (me & ~1) + jnp.arange(2, dtype=jnp.int32)
    first_rows = jnp.take(tile_slab, buckets, axis=0) * SLAB_ROWS + jnp.take(tile_row, buckets, axis=0)
    target = (first_rows[:, :, None] + within).reshape(2, -1)
    slab_order = list(range(slab_count - 1, -1, -1))
    wanted = jnp.concatenate(
        [(here ^ r) * SLAB_ROWS + jnp.arange(SLAB_ROWS, dtype=jnp.int32) for r in slab_order]
    )[:, None]
    late_logs, mixing = matrix(me_ref, wanted, target, early_weights, late_scores, got_late, capacity, score_scale)

    count = slab_count // 2
    middle = SLAB_ROWS // 2
    bits = list(range(1, orient_count.bit_length() - 1))
    split, stage, sums = {}, {}, {}

    def keep(n, token):
        which = mixing if token is None else after(mixing, token)
        split[n] = mix(me_ref, which, n, pieces, orient_count)
        return split[n][1]

    def begin(n, token):
        state = tuple(split[n])
        if token is not None:
            state = after(state, token)
        stage[n] = exchange(state, 0, bits)

    def advance(n, step, token):
        landed, upper, lower = stage[n]
        state = add_split(after(landed, token), upper, lower)
        if n + 1 == count and step + 1 == len(bits):
            stage[n] = [
                exchange(tuple(x[:, begin : begin + middle] for x in state), step, bits)
                for begin in (0, middle)
            ]
        else:
            stage[n] = exchange(state, step, bits)
        return state[1]

    def gathered(n, token, tie=None):
        for step in range(2, len(bits)):
            token = advance(n, step, token)
        if n + 1 == count:
            totals = []
            for k, (landed, upper, lower) in enumerate(stage[n]):
                landed = after(landed, (token, tie) if k == 0 else token)
                token = jnp.concatenate(
                    [upper[0] + landed[0][0].astype(F32), lower[0] + landed[1][0].astype(F32)]
                )
                totals.append(token)
            return totals
        landed, upper, lower = stage[n]
        landed = after(landed, token)
        upper = upper[0] + landed[0][0].astype(F32)
        lower = lower[0] + landed[1][0].astype(F32)
        return [
            jnp.concatenate([upper[:middle], lower[:middle]]),
            jnp.concatenate([upper[middle:], lower[middle:]]),
        ]

    def deliver(n, totals):
        for total, offset in zip(totals, slab_order[2 * n : 2 * n + 2]):
            for block in sums.get(offset, []):
                total = total + block.astype(F32)
            if offset:
                step = offset & -offset
                token = total.astype(BF16)
                sums.setdefault(offset ^ step, []).append(swap(token, "slab", step))
        return total, token

    token = keep(0, None)
    begin(0, None)
    for n in range(count):
        if n + 1 < count:
            token = keep(n + 1, token)
        landed = stage[n][0]
        token = advance(n, 1, token)
        if n + 1 < count:
            begin(n + 1, landed)
        totals = gathered(n, token, sums[0] if n + 1 == count else None)
        volume, token = deliver(n, totals)
    logs = jnp.concatenate([early_logs, late_logs], axis=1)[:, :, 0]
    logs = lax.dynamic_index_in_dim(logs, me & 1, 0, keepdims=False)
    logsum = after(logs.reshape(orient_count, capacity), token)
    logsum = jnp.stack([logsum[order.index(r)] for r in range(orient_count)])
    logsum = jnp.take(logsum, me ^ jnp.arange(orient_count, dtype=jnp.int32), axis=0)
    returned = lax.all_to_all(logsum[:, None, :], "orient", split_axis=0, concat_axis=0, tiled=True)
    place = slot_of[None, :] == jnp.arange(orient_count * capacity, dtype=jnp.int32)[:, None]
    loglik = jnp.sum(jnp.where(place, returned.reshape(-1)[:, None], 0.0), axis=0)
    return (volume, loglik)


def solution(mesh):
    in_specs = (
        P(("orient", "slab"), None),
        P(("orient", "slab"), None),
        P("orient", None, None),
        P(),
        P(),
    )
    out_specs = (P("slab", "orient"), P(("orient", "slab")))
    return jax.shard_map(body, mesh=mesh, in_specs=in_specs, out_specs=out_specs, check_vma=False)
```

```python
import functools
import math

import jax
import jax.numpy as jnp
from jax import lax
from jax.experimental import pallas as pl
from jax.experimental.pallas import tpu as pltpu
from jax.sharding import PartitionSpec as P

G = 8
SLAB_ROWS = 256
BETA = 2.0
F32 = jnp.float32
BF16 = jnp.bfloat16
VMEM_LIMIT = 16 * 1024 * 1024


def slots(labels, groups, capacity):
    onehot = (labels[:, None] == jnp.arange(groups, dtype=jnp.int32)[None, :]).astype(jnp.int32)
    ordinal = jnp.sum((jnp.cumsum(onehot, axis=0) - 1) * onehot, axis=1)
    return labels * capacity + ordinal


def after(x, token):
    return lax.optimization_barrier((x, token))[0]


def swap(x, axis, offset):
    count = lax.axis_size(axis)
    return lax.ppermute(x, axis, [(i, i ^ offset) for i in range(count)])


def call(kernel, name, grid, in_specs, out_specs, out_shape, scratch, flops, size):
    return pl.pallas_call(
        kernel,
        name=name,
        grid_spec=pltpu.PrefetchScalarGridSpec(
            num_scalar_prefetch=1,
            grid=grid,
            in_specs=in_specs,
            out_specs=out_specs,
            scratch_shapes=scratch,
        ),
        out_shape=out_shape,
        compiler_params=pltpu.CompilerParams(vmem_limit_bytes=VMEM_LIMIT),
        cost_estimate=pl.CostEstimate(flops=20 * flops, bytes_accessed=20 * size, transcendentals=0),
    )


def gather_kernel(chips, capacity, owned, me_ref, slot_ref, images_ref, *rest):
    outs, select = rest[:-1], rest[-1]
    low, chip = me_ref[0] & 1, me_ref[0] >> 1
    both = 2 * capacity

    @pl.when(pl.program_id(0) == 0)
    def _():
        row = lax.broadcasted_iota(jnp.int32, (both, slot_ref.shape[1]), 0)
        for n, offset in enumerate(chips):
            hit = slot_ref[...] == row + (chip ^ offset) * both
            select[n * both : (n + 1) * both, :] = hit.astype(BF16)

    for which in range(2):
        block = images_ref[:, which * owned : (which + 1) * owned]
        found = jnp.dot(select[...], block, preferred_element_type=F32).astype(BF16)
        for core in range(2):

            @pl.when(low == core)
            def _():
                for n in range(len(chips)):
                    for member in range(2):
                        begin = n * both + member * capacity
                        rows = found[begin : begin + capacity]
                        out = 2 * n + (which ^ core)
                        outs[2 * out + member][...] = rows


def gather(chips, me, slot_of, images, orient_count, capacity):
    rows, window = images.shape
    owned = window // orient_count
    count = 4 * len(chips)
    outs = call(
        functools.partial(gather_kernel, chips, capacity, owned),
        "gather",
        (orient_count // 2,),
        [
            pl.BlockSpec((1, rows), lambda j, me: (0, 0)),
            pl.BlockSpec((rows, 2 * owned), lambda j, me: (0, j)),
        ],
        [pl.BlockSpec((capacity, owned), lambda j, me: (0, j))] * count,
        [jax.ShapeDtypeStruct((capacity, window // 2), BF16)] * count,
        [pltpu.VMEM((2 * len(chips) * capacity, rows), BF16)],
        4 * len(chips) * capacity * rows * window,
        2 * window * (rows + 2 * len(chips) * capacity),
    )(me, slot_of, images)
    offsets = [2 * q + swapped for q in chips for swapped in range(2)]
    return {r: [outs[2 * n], outs[2 * n + 1]] for n, r in enumerate(offsets)}


def copy_kernel(me_ref, panel_ref, out_ref):
    out_ref[...] = panel_ref[...]


def partner_columns(me, panel, orient_count):
    rows, window = panel.shape
    owned = window // orient_count
    return call(
        copy_kernel,
        "partner_columns",
        (orient_count // 2,),
        [pl.BlockSpec((rows, owned), lambda j, me: (0, 2 * j + 1 - (me[0] & 1)))],
        pl.BlockSpec((rows, owned), lambda j, me: (0, j)),
        jax.ShapeDtypeStruct((rows, window // 2), BF16),
        [],
        0,
        2 * rows * window,
    )(me, panel)


def score_kernel(members, count, me_ref, mine_ref, other_ref, *rest):
    rows, out_ref = rest[:-1], rest[-1]
    low = me_ref[0] & 1
    for n, member in enumerate(members):
        block = jnp.concatenate([ref[...] for ref in rows[n * count : (n + 1) * count]], axis=0)
        panel = jnp.where(low == member, mine_ref[...], other_ref[...])
        term = lax.dot_general(
            block, panel, (((1,), (1,)), ((), ())), preferred_element_type=F32
        )

        @pl.when(pl.program_id(0) == 0)
        def _():
            out_ref[n] = term

        @pl.when(pl.program_id(0) > 0)
        def _():
            out_ref[n] += term


def score(members, me, panel, other, pieces, orient_count):
    rows = [piece[member] for member in members for piece in pieces]
    orient_total, window = panel.shape
    owned = window // orient_count
    capacity = rows[0].shape[0]
    shape = (len(members), len(pieces) * capacity, orient_total)
    return call(
        functools.partial(score_kernel, members, len(pieces)),
        "score",
        (orient_count // 2,),
        [
            pl.BlockSpec((orient_total, owned), lambda j, me: (0, 2 * j + (me[0] & 1))),
            pl.BlockSpec((orient_total, owned), lambda j, me: (0, j)),
        ]
        + [pl.BlockSpec((capacity, owned), lambda j, me: (0, j))] * len(rows),
        pl.BlockSpec(shape, lambda j, me: (0, 0, 0)),
        jax.ShapeDtypeStruct(shape, F32),
        [],
        shape[0] * shape[1] * orient_total * window,
        2 * window * (orient_total + shape[1]),
    )(me, panel, other, *rows)


def softmax(mine, got, capacity, scale):
    count = got.shape[0] // capacity
    got = jnp.concatenate(
        [got[(n ^ 1) * capacity : ((n ^ 1) + 1) * capacity] for n in range(count)], axis=0
    )
    scores = (mine + got) * scale
    largest = jnp.max(scores, axis=1, keepdims=True)
    exponent = jnp.exp(scores - largest)
    totals = jnp.sum(exponent, axis=1, keepdims=True)
    return (exponent / totals).astype(BF16), largest + jnp.log(totals)


def weigh_kernel(capacity, scale, me_ref, mine_ref, got_ref, weight_ref, logsum_ref):
    weight_ref[0], logsum_ref[0] = softmax(mine_ref[0], got_ref[0], capacity, scale)


def weigh(me, mine, got, capacity, scale):
    members, rows, orient_total = mine.shape
    block = pl.BlockSpec((1, rows, orient_total), lambda j, me: (j, 0, 0))
    return call(
        functools.partial(weigh_kernel, capacity, scale),
        "weigh",
        (members,),
        [block, block],
        [block, pl.BlockSpec((1, rows, 1), lambda j, me: (j, 0, 0))],
        [
            jax.ShapeDtypeStruct(mine.shape, BF16),
            jax.ShapeDtypeStruct((members, rows, 1), F32),
        ],
        [],
        10 * members * rows * orient_total,
        10 * members * rows * orient_total,
    )(me, mine, got)


def matrix_kernel(capacity, scale, me_ref, wanted_ref, target_ref, early_ref, *rest):
    mine, got, (logsum_ref, mix_ref, joined) = rest[:2], rest[2:4], rest[4:]
    early = early_ref.shape[1]
    late = mine[0].shape[1]
    for member in range(2):
        joined[:early, :] = early_ref[member]
        joined[early:, :], logsum_ref[member] = softmax(
            mine[member][0], got[member][0], capacity, scale
        )
        weights = joined[...]
        for n in range(wanted_ref.shape[0] // SLAB_ROWS):
            rows = slice(n * SLAB_ROWS, (n + 1) * SLAB_ROWS)
            spread = (wanted_ref[rows, :] == target_ref[member : member + 1, :]).astype(BF16)
            mix_ref[rows, member * (early + late) : (member + 1) * (early + late)] = lax.dot_general(
                spread, weights, (((1,), (1,)), ((), ())), preferred_element_type=F32
            ).astype(BF16)


def matrix(me, wanted, target, early, mine, got, capacity, scale):
    volume_rows = wanted.shape[0]
    _, late, orient_total = mine[0].shape
    particles = early.shape[1] + late

    def whole(shape):
        return pl.BlockSpec(shape, lambda j, me: (0,) * len(shape))

    return call(
        functools.partial(matrix_kernel, capacity, scale),
        "matrix",
        (1,),
        [whole(x.shape) for x in (wanted, target, early, *mine, *got)],
        [whole((2, late, 1)), whole((volume_rows, 2 * particles))],
        [
            jax.ShapeDtypeStruct((2, late, 1), F32),
            jax.ShapeDtypeStruct((volume_rows, 2 * particles), BF16),
        ],
        [pltpu.VMEM((particles, orient_total), BF16)],
        4 * volume_rows * particles * orient_total,
        4 * volume_rows * particles,
    )(me, wanted, target, early, *mine, *got)


def mix_kernel(count, blocks, me_ref, mix_ref, *rest):
    rows = rest[:count]
    upper_sent, upper_kept, lower_sent, lower_kept, stacked = rest[count:]
    step = pl.program_id(0)
    begin = 0
    for ref in rows:
        stacked[begin : begin + ref.shape[0], :] = ref[...]
        begin += ref.shape[0]
    total = jnp.dot(mix_ref[...], stacked[...], preferred_element_type=F32)
    middle = SLAB_ROWS // 2
    parts = [total[begin : begin + middle] for begin in range(0, total.shape[0], middle)]
    upper = jnp.concatenate(parts[0::2], axis=0)
    lower = jnp.concatenate(parts[1::2], axis=0)

    @pl.when(step % 2 == 1)
    def _():
        upper_sent[step // 2] = upper.astype(BF16)

    @pl.when(step % 2 == 0)
    def _():
        upper_kept[step // 2] = upper

    @pl.when(step >= blocks // 2)
    def _():
        lower_sent[step % (blocks // 2)] = lower.astype(BF16)

    @pl.when(step < blocks // 2)
    def _():
        lower_kept[step % (blocks // 2)] = lower


def mix(me, matrix, place, pieces, orient_count):
    rows = [piece[member] for member in range(2) for piece in pieces]
    particles = matrix.shape[1]
    half = rows[0].shape[1]
    blocks = orient_count // 2
    owned = half // blocks
    volume_rows = 2 * SLAB_ROWS
    part = (blocks // 2, SLAB_ROWS, owned)
    return call(
        functools.partial(mix_kernel, len(rows), blocks),
        "mix",
        (blocks,),
        [pl.BlockSpec((volume_rows, particles), lambda j, me: (place, 0))]
        + [pl.BlockSpec((r.shape[0], owned), lambda j, me: (0, (me[0] >> 1) ^ j)) for r in rows],
        [pl.BlockSpec(part, lambda j, me: (0, 0, 0))] * 4,
        [jax.ShapeDtypeStruct(part, BF16), jax.ShapeDtypeStruct(part, F32)] * 2,
        [pltpu.VMEM((particles, owned), BF16)],
        2 * volume_rows * particles * half,
        2 * half * (particles + volume_rows),
    )(me, matrix, *rows)


def exchange(state, n, bits):
    upper_sent, upper_kept, lower_sent, lower_kept = state
    got = (
        swap(upper_sent, "orient", 1 << bits[n]),
        swap(lower_sent, "orient", 1 << bits[-1 - n]),
    )
    return got, upper_kept, lower_kept


def add_split(got, upper_kept, lower_kept):
    upper = upper_kept + got[0].astype(F32)
    lower = lower_kept + got[1].astype(F32)
    middle = (lower.shape[0] + 1) // 2
    return upper[1::2].astype(BF16), upper[0::2], lower[middle:].astype(BF16), lower[:middle]


def body(images, bucket, panels, tile_slab, tile_row):
    orient_count = lax.axis_size("orient")
    slab_count = lax.axis_size("slab")
    me = lax.axis_index("orient")
    here = lax.axis_index("slab")
    me_ref = me.astype(jnp.int32).reshape(1)
    per_device, window = images.shape
    capacity = 2 * per_device // orient_count
    panel = panels[0]
    score_scale = BETA / math.sqrt(window)

    slot_of = slots(bucket[:, 0], orient_count, capacity)
    slot_row = slot_of[None, :]

    chips = sorted(range(1, orient_count // 2), key=lambda q: (-q.bit_count(), q))
    far, near = chips[:-2], chips[-2:]
    outgoing = gather(far[:1], me_ref, slot_row, images, orient_count, capacity)
    early = [0, 1] + [2 * q + swapped for q in far for swapped in range(2)]
    late = [2 * q + swapped for q in near for swapped in range(2)]
    order = early + late
    arrived = {}
    for offset in early[2:4]:
        arrived[offset] = [swap(half, "orient", offset) for half in outgoing[offset]]
    images, panel_ready = after((images, panel), (arrived[early[2]][0], arrived[early[3]][0]))
    sent_panel = partner_columns(me_ref, panel_ready, orient_count)
    outgoing |= gather([0] + chips[1:], me_ref, slot_row, images, orient_count, capacity)
    arrived[0] = outgoing[0]
    for offset in early[4:] + early[1:2] + [2 * q + swapped for swapped in range(2) for q in near]:
        arrived[offset] = [swap(half, "orient", offset) for half in outgoing[offset]]
    pieces = [arrived[r] for r in order]

    other = swap(sent_panel, "orient", 1)
    early_pieces, late_pieces = pieces[: len(early)], pieces[len(early) :]
    early_scores = score((0, 1), me_ref, panel, other, early_pieces, orient_count)
    early_weights, early_logs = weigh(
        me_ref, early_scores, swap(early_scores, "orient", 1), capacity, score_scale
    )
    late_scores, got_late = [], []
    for member in range(2):
        if member == 1:
            other = after(other, early_weights)
        found = score((member,), me_ref, panel, other, late_pieces, orient_count)
        late_scores.append(found)
        got_late.append(swap(found, "orient", 1))

    within = jnp.arange(G, dtype=jnp.int32)
    buckets = (me & ~1) + jnp.arange(2, dtype=jnp.int32)
    first_rows = jnp.take(tile_slab, buckets, axis=0) * SLAB_ROWS + jnp.take(tile_row, buckets, axis=0)
    target = (first_rows[:, :, None] + within).reshape(2, -1)
    slab_order = list(range(slab_count - 1, -1, -1))
    wanted = jnp.concatenate(
        [(here ^ r) * SLAB_ROWS + jnp.arange(SLAB_ROWS, dtype=jnp.int32) for r in slab_order]
    )[:, None]
    late_logs, mixing = matrix(me_ref, wanted, target, early_weights, late_scores, got_late, capacity, score_scale)

    count = slab_count // 2
    middle = SLAB_ROWS // 2
    bits = list(range(1, orient_count.bit_length() - 1))
    split, stage, sums = {}, {}, {}

    def keep(n, token):
        which = mixing if token is None else after(mixing, token)
        split[n] = mix(me_ref, which, n, pieces, orient_count)
        return split[n][1]

    def begin(n, token):
        state = tuple(split[n])
        if token is not None:
            state = after(state, token)
        stage[n] = exchange(state, 0, bits)

    def advance(n, step, token):
        landed, upper, lower = stage[n]
        state = add_split(after(landed, token), upper, lower)
        if n + 1 == count and step + 1 == len(bits):
            stage[n] = [
                exchange(tuple(x[:, begin : begin + middle] for x in state), step, bits)
                for begin in (0, middle)
            ]
        else:
            stage[n] = exchange(state, step, bits)
        return state[1]

    def gathered(n, token, tie=None):
        for step in range(2, len(bits)):
            token = advance(n, step, token)
        if n + 1 == count:
            totals = []
            for k, (landed, upper, lower) in enumerate(stage[n]):
                landed = after(landed, (token, tie) if k == 0 else token)
                token = jnp.concatenate(
                    [upper[0] + landed[0][0].astype(F32), lower[0] + landed[1][0].astype(F32)]
                )
                totals.append(token)
            return totals
        landed, upper, lower = stage[n]
        landed = after(landed, token)
        upper = upper[0] + landed[0][0].astype(F32)
        lower = lower[0] + landed[1][0].astype(F32)
        return [
            jnp.concatenate([upper[:middle], lower[:middle]]),
            jnp.concatenate([upper[middle:], lower[middle:]]),
        ]

    def deliver(n, totals):
        for total, offset in zip(totals, slab_order[2 * n : 2 * n + 2]):
            for block in sums.get(offset, []):
                total = total + block.astype(F32)
            if offset:
                step = offset & -offset
                token = total.astype(BF16)
                sums.setdefault(offset ^ step, []).append(swap(token, "slab", step))
        return total, token

    token = keep(0, None)
    begin(0, None)
    for n in range(count):
        if n + 1 < count:
            token = keep(n + 1, token)
        landed = stage[n][0]
        token = advance(n, 1, token)
        if n + 1 < count:
            begin(n + 1, landed)
        totals = gathered(n, token, sums[0] if n + 1 == count else None)
        volume, token = deliver(n, totals)
    logs = jnp.concatenate([early_logs, late_logs], axis=1)[:, :, 0]
    logs = lax.dynamic_index_in_dim(logs, me & 1, 0, keepdims=False)
    logsum = after(logs.reshape(orient_count, capacity), token)
    logsum = jnp.stack([logsum[order.index(r)] for r in range(orient_count)])
    logsum = jnp.take(logsum, me ^ jnp.arange(orient_count, dtype=jnp.int32), axis=0)
    returned = lax.all_to_all(logsum[:, None, :], "orient", split_axis=0, concat_axis=0, tiled=True)
    place = slot_of[None, :] == jnp.arange(orient_count * capacity, dtype=jnp.int32)[:, None]
    loglik = jnp.sum(jnp.where(place, returned.reshape(-1)[:, None], 0.0), axis=0)
    return (volume, loglik)


def solution(mesh):
    in_specs = (
        P(("orient", "slab"), None),
        P(("orient", "slab"), None),
        P("orient", None, None),
        P(),
        P(),
    )
    out_specs = (P("slab", "orient"), P(("orient", "slab")))
    return jax.shard_map(body, mesh=mesh, in_specs=in_specs, out_specs=out_specs, check_vma=False)
```
